32 devices in a mesh: row: 8 (over z, x), col: 4 (over y, core).
Axes of the slice: x: 2, y: 2, z: 4, core: 2. Of those that a mesh axis runs over, the one named last changes fastest.
Arguments:
- panel: bfloat16 [1024, 18432], P('col', 'row'), may hold values from -6 to 6
- mask: int32 [1024], P('row'), may hold values 0 or 1
- timesteps: int32 [1], replicated, may hold values from 3 to 31
- cot_gate: bfloat16 [1024, 36864], P('row', 'col'), may hold values from -6 to 6
Outputs:
- grad_gate: float32 [18432, 36864], P('row', 'col')
The draws below stay inside these ranges and needn't reach their ends.
All inputs are finite; a program needn't handle non-finite values. No bound on the sum of `mask` on one device may be relied on, other than what follows from the above.
Results may differ from the reference program's by a relative error of at most 0.0027.
Values may be sent and summed in bfloat16 or wider, within the bound.
No kernel may reach another device: no remote copies, remote signals or barrier semaphores. Data moves between devices by JAX's collectives and lax.ppermute only.
A program may use at most 256 MiB of HBM per device.

```python
import math
import jax
import jax.numpy as jnp
from jax import lax

FF_WIN = 36864
STEPS = 32
SEQS = 1
KWIN = 18432
TOKENS = 1024
N_COL = 4


def set_ends(entries, stream_key, low, high):
    shape = entries.shape
    place = [jax.random.randint(jax.random.fold_in(stream_key, axis), (), 0, shape[axis]) for axis in range(len(shape))]
    entries = entries.at[tuple(place)].set(low)
    longest = shape.index(max(shape))
    place[longest] = (place[longest] + 1) % shape[longest]
    return entries.at[tuple(place)].set(high)


def raised(values, rng, source, target, blocks, factor):
    def block_of(dim):
        return (jnp.arange(values.shape[dim]) // (values.shape[dim] // blocks)).reshape((-1,) + (1,) * (values.ndim - 1 - dim))

    one_side = jax.random.permutation(rng, blocks)[block_of(target)]
    other_side = (block_of(target) + blocks // 2) % blocks
    return jnp.where((block_of(source) == one_side) | (block_of(source) == other_side), factor * values, values)


def level_of(own_key, shape, split, low, high):
    def one(axis_at, parts):
        heights = jax.random.uniform(jax.random.fold_in(jax.random.fold_in(own_key, 6), axis_at), (parts,), jnp.float32, low / len(split), high / len(split))
        return jnp.repeat(jnp.exp(heights), shape[axis_at] // parts).reshape((-1,) + (1,) * (len(shape) - axis_at - 1))

    gain = one(*split[0])
    for cut in split[1:]:
        gain = gain * one(*cut)
    return gain


def bell_draw(rng, shape, spread, bound, shards=(), kind=jnp.bfloat16):
    values = spread * jax.random.normal(rng, shape, jnp.float32)
    if shards:
        values = values * level_of(rng, shape, shards, -0.22, 0.18)
    return jnp.clip(values, -bound, bound).astype(kind)


def gaussian_with(rng, shape, scale, reach, shards, heavy, held_as=jnp.bfloat16):
    values = scale * jax.random.normal(rng, shape, jnp.float32)
    if shards:
        values = values * level_of(rng, shape, shards, -0.22, 0.18)
    return jnp.clip(raised(values, jax.random.fold_in(rng, 3), *heavy), -reach, reach).astype(held_as)


def setup_inputs(seed: int = 0) -> dict:
    keys = jax.random.split(jax.random.key(seed), 5)
    panel = gaussian_with(keys[0], (TOKENS, KWIN), 1.0, 6.0, ((0, 4), (1, 8)), (0, 1, 8, 2.0))
    mask = set_ends((jax.random.randint(keys[1], (TOKENS,), 0, 2) < 1).astype(jnp.int32), jax.random.fold_in(keys[1], 1), 0, 1)
    timesteps = jax.random.randint(keys[2], (SEQS,), 3, STEPS).astype(jnp.int32)
    cot_gate = bell_draw(keys[3], (TOKENS, FF_WIN), 1.0, 6.0, ((0, 8), (1, 4)))
    return {"panel": panel, "mask": mask, "timesteps": timesteps, "cot_gate": cot_gate}


def token_weights(mask, timesteps, first, seq_len, total):
    count = mask.shape[0]
    position = first + jnp.arange(count, dtype=jnp.int32)
    which = position // seq_len
    onehot = which[:, None] == jnp.arange(timesteps.shape[0], dtype=jnp.int32)[None, :]
    level = lax.optimization_barrier(jnp.sum(jnp.where(onehot, timesteps[None, :], 0), axis=1))
    scale = 1.0 / math.sqrt(total)
    return mask.astype(jnp.float32) * (STEPS / (level + 1).astype(jnp.float32)) * scale

def reference(panel, mask, timesteps, cot_gate):
    weights = token_weights(mask, timesteps, 0, TOKENS // SEQS, TOKENS)
    weighted = (cot_gate.astype(jnp.float32) * weights[:, None]).astype(jnp.bfloat16)
    width = FF_WIN // N_COL
    dims = (((0,), (0,)), ((), ()))

    def column_block(index):
        first = (index * width).astype(jnp.int32)
        slab = lax.dynamic_slice_in_dim(weighted, first, width, 1)
        return lax.dot_general(panel, slab, dims, preferred_element_type=jnp.float32)
    stacked = lax.map(column_block, jnp.arange(N_COL, dtype=jnp.int32))
    return jnp.transpose(stacked, (1, 0, 2)).reshape(KWIN, FF_WIN)
```

```python
import functools
import math

import jax
import jax.numpy as jnp
from jax import lax
from jax.experimental import pallas as pl
from jax.experimental.pallas import tpu as pltpu
from jax.sharding import PartitionSpec as P

STEPS = 32
LANES = 128
CAPS = (64, 80, 96, 128)
SPLIT = (2, 2, 2)


def token_weights(mask, timesteps, first, seq_len, total):
    count = mask.shape[0]
    position = first + jnp.arange(count, dtype=jnp.int32)
    which = position // seq_len
    onehot = which[:, None] == jnp.arange(timesteps.shape[0], dtype=jnp.int32)[None, :]
    level = jnp.sum(jnp.where(onehot, timesteps[None, :], 0), axis=1)
    scale = 1.0 / math.sqrt(total)
    return mask.astype(jnp.float32) * (STEPS / (level + 1).astype(jnp.float32)) * scale


def cycle(n):
    fast = 1
    while fast * fast * 4 <= n:
        fast *= 2
    slow = n // fast
    walk = [z * fast for z in range(slow)]
    for i, z in enumerate(reversed(range(slow))):
        xs = range(1, fast) if i % 2 == 0 else reversed(range(1, fast))
        walk += [z * fast + x for x in xs]
    return walk


def chunks_of(width):
    tiles = width // LANES
    fore = (tiles + 1) // 2
    out = []
    for first, count in ((0, fore), (fore, tiles - fore)):
        total = sum(SPLIT)
        parts = SPLIT if count % total == 0 and tiles % 2 == 0 else (total,)
        unit = count // total if len(parts) > 1 else 0
        ranges, at = [], first
        for part in parts:
            size = part * unit if len(parts) > 1 else count
            ranges.append((at * LANES, size * LANES))
            at += size
        out.append(ranges)
    return out


def tile_of(first, width, most):
    size = math.gcd(first, width) if first else width
    best = LANES
    for k in range(1, most // LANES + 1):
        if size % (k * LANES) == 0:
            best = k * LANES
    return best


def product_kernel(n, cap, slot, panel_ref, *refs):
    pieces, out_ref, depth_ref = refs[:n], refs[-2], refs[-1]

    @pl.when(pl.program_id(1) == 0)
    def _():
        for j in range(n):
            depth_ref[j * slot : j * slot + cap, :] = pieces[j][...]
            if slot > cap:
                depth_ref[j * slot + cap : (j + 1) * slot, :] = jnp.zeros(
                    (slot - cap, depth_ref.shape[1]), depth_ref.dtype
                )

    out_ref[...] = jnp.dot(panel_ref[0], depth_ref[...], preferred_element_type=jnp.float32)


def product(panel_t, pieces, out, first, shape):
    n, (cap, width) = len(pieces), pieces[0].shape
    blocks, rows, depth = panel_t.shape
    slot = depth // n
    tile = tile_of(first, width, 768)
    base = first // tile
    specs = [pl.BlockSpec((1, rows, depth), lambda j, i: (i, 0, 0))]
    specs += [pl.BlockSpec((cap, tile), lambda j, i: (0, j)) for _ in pieces]
    args = [panel_t, *pieces]
    aliases = {}
    if out is not None:
        specs.append(pl.BlockSpec(memory_space=pl.ANY))
        args.append(out)
        aliases = {len(args) - 1: 0}
    return pl.pallas_call(
        functools.partial(product_kernel, n, cap, slot),
        grid=(width // tile, blocks),
        in_specs=specs,
        out_specs=pl.BlockSpec((rows, tile), lambda j, i: (i, base + j)),
        out_shape=jax.ShapeDtypeStruct(shape, jnp.float32),
        scratch_shapes=[pltpu.VMEM((depth, tile), jnp.bfloat16)],
        input_output_aliases=aliases,
        compiler_params=pltpu.CompilerParams(vmem_limit_bytes=48 * 2**20),
        cost_estimate=pl.CostEstimate(
            flops=2 * blocks * rows * depth * width,
            bytes_accessed=blocks * rows * (4 * width + 2 * depth) + 2 * n * cap * width,
            transcendentals=0,
        ),
    )(*args)


def gather_and_multiply(cap, walk, compact, panel, masks):
    n, per = masks.shape
    features = panel.shape[1]
    shape = (features, compact.shape[1])
    fore = [(walk[i], walk[(i + 1) % n]) for i in range(n)]
    back = [(b, a) for a, b in fore]
    slot = -(-cap // 16) * 16

    place = jnp.argmax(jnp.asarray(walk) == lax.axis_index("row"))
    owner = jnp.asarray(walk, dtype=jnp.int32)[(place - jnp.arange(n)) % n]
    rank = jnp.where(masks > 0, jnp.cumsum(masks, axis=1) - 1, -1)
    there = owner[:, None] == jnp.arange(n)[None, :]
    pick = there[:, None, :, None] & (rank[None, None] == jnp.arange(slot)[None, :, None, None])
    pick = pick.astype(jnp.bfloat16).reshape(n * slot, n * per)
    blocks = 1
    for b in (3, 2):
        if features % (b * LANES) == 0:
            blocks = b
            break
    panel_t = lax.dot_general(
        panel, pick, (((0,), (1,)), ((), ())), preferred_element_type=jnp.float32
    ).astype(jnp.bfloat16)
    panel_t = panel_t.reshape(blocks, features // blocks, n * slot)

    out = None
    ahead, behind = chunks_of(compact.shape[1])
    for k in range(max(len(ahead), len(behind))):
        for ranges, perm, sign in ((ahead, fore, 1), (behind, back, -1)):
            if k >= len(ranges):
                continue
            first, width = ranges[k]
            piece = compact[:cap, first : first + width]
            pieces = [piece] + [None] * (n - 1)
            for s in range(1, n):
                piece = lax.ppermute(piece, "row", perm)
                pieces[(sign * s) % n] = piece
            out = product(panel_t, pieces, out, first, shape)
    return out


def body(panel, mask, timesteps, cot_gate):
    n = lax.axis_size("row")
    per = cot_gate.shape[0]
    total = per * n
    seq_len = total // timesteps.shape[0]
    first = lax.axis_index("row") * per
    masks = lax.all_gather(mask, "row", axis=0, tiled=False)
    whole_panel = lax.all_gather(panel, "col", axis=0, tiled=True)
    weights = token_weights(mask, timesteps, first, seq_len, total)
    weighted = (cot_gate.astype(jnp.float32) * weights[:, None]).astype(jnp.bfloat16)
    rank = jnp.where(mask > 0, jnp.cumsum(mask) - 1, -1)
    pick = (rank[None, :] == jnp.arange(per)[:, None]).astype(jnp.bfloat16)
    compact = jnp.dot(pick, weighted, preferred_element_type=jnp.float32).astype(jnp.bfloat16)

    caps = [c for c in CAPS if c < per] + [per]
    most = jnp.max(jnp.sum(masks, axis=1))
    which = jnp.sum(most > jnp.asarray(caps[:-1], dtype=jnp.int32)).astype(jnp.int32)
    walk = cycle(n)
    branches = [functools.partial(gather_and_multiply, cap, walk) for cap in caps]
    return lax.switch(which, branches, compact, whole_panel, masks)


def solution(mesh):
    placed = (P("col", "row"), P("row"), P(), P("row", "col"))
    return jax.shard_map(
        body, mesh=mesh, in_specs=placed, out_specs=P("row", "col"), check_vma=False
    )
```

```python
import functools
import math

import jax
import jax.numpy as jnp
import numpy as np
from jax import lax
from jax.experimental import pallas as pl
from jax.experimental.pallas import tpu as pltpu
from jax.sharding import PartitionSpec as P

STEPS = 32
LANES = 128
ROWS = 80
SPLIT = (2, 4)
TIGHT = True
STAGGER = 3
LIMIT = 28 * 2**20


def token_weights(mask, timesteps, first, seq_len, total):
    count = mask.shape[0]
    position = first + jnp.arange(count, dtype=jnp.int32)
    which = position // seq_len
    onehot = which[:, None] == jnp.arange(timesteps.shape[0], dtype=jnp.int32)[None, :]
    level = jnp.sum(jnp.where(onehot, timesteps[None, :], 0), axis=1)
    scale = 1.0 / math.sqrt(total)
    return mask.astype(jnp.float32) * (STEPS / (level + 1).astype(jnp.float32)) * scale


def cycle(n):
    fast = 1
    while fast * fast * 4 <= n:
        fast *= 2
    slow = n // fast
    walk = [z * fast for z in range(slow)]
    for i, z in enumerate(reversed(range(slow))):
        xs = range(1, fast) if i % 2 == 0 else reversed(range(1, fast))
        walk += [z * fast + x for x in xs]
    return walk


def chunks_of(width, split):
    tiles = width // LANES
    fore = (tiles + 1) // 2
    out = []
    for first, count in ((0, fore), (fore, tiles - fore)):
        if tiles % 2 or count % sum(split):
            split = (1,)
        ranges, at = [], first
        for part in split:
            size = part * (count // sum(split))
            ranges.append((at * LANES, size * LANES))
            at += size
        out.append(ranges)
    return out


def tile_of(first, width, most):
    best = LANES
    for size in range(LANES, most + 1, LANES):
        if first % size == 0 and width % size == 0:
            best = size
    return best


def picker(mask_row, base, rows):
    count = mask_row.shape[1]
    kept = jnp.broadcast_to(mask_row, (8, count)).astype(jnp.float32)
    before = lax.broadcasted_iota(jnp.int32, (count, count), 0)
    after = lax.broadcasted_iota(jnp.int32, (count, count), 1)
    upper = jnp.where(before <= after, 1.0, 0.0)
    rank = jnp.dot(kept.astype(jnp.bfloat16), upper.astype(jnp.bfloat16), preferred_element_type=jnp.float32)
    rank = jnp.where(kept > 0, rank, 0.0)[0:1]
    place = lax.broadcasted_iota(jnp.int32, (rows, count), 0) + (base + 1)
    return jnp.where(place.astype(jnp.float32) == rank, 1.0, 0.0).astype(jnp.bfloat16)


def pack_kernel(base, rows, unit, ranges, mask_ref, weight_ref, cot_ref, *outs):
    count = cot_ref.shape[0]
    pick = picker(mask_ref[...], base, rows)
    across = lax.broadcasted_iota(jnp.int32, (count, count), 0)
    along = lax.broadcasted_iota(jnp.int32, (count, count), 1)
    weight = jnp.sum(jnp.where(across == along, weight_ref[...], 0.0), axis=1, keepdims=True)
    weighted = (cot_ref[...].astype(jnp.float32) * weight).astype(jnp.bfloat16)
    packed = jnp.dot(pick, weighted, preferred_element_type=jnp.float32).astype(jnp.bfloat16)
    steps = [width // unit for _, width in ranges]
    for k, out in enumerate(outs):
        for u in range(steps[k]):

            @pl.when(pl.program_id(0) == sum(steps[:k]) + u)
            def _(out=out, u=u):
                out[:, u * unit : (u + 1) * unit] = packed


def pack(cot, mask, weights, base, rows, ranges):
    count = cot.shape[0]
    unit = functools.reduce(math.gcd, [v for r in ranges for v in r if v])
    (first, width), (second, other) = ranges
    steps = width // unit
    return pl.pallas_call(
        functools.partial(pack_kernel, base, rows, unit, ranges),
        grid=((width + other) // unit,),
        in_specs=[
            pl.BlockSpec((1, count), lambda i: (0, 0)),
            pl.BlockSpec((1, count), lambda i: (0, 0)),
            pl.BlockSpec(
                (count, unit),
                lambda i: (0, jnp.where(i < steps, first // unit + i, second // unit + i - steps)),
            ),
        ],
        out_specs=[pl.BlockSpec((rows, w), lambda i: (0, 0)) for _, w in ranges],
        out_shape=[jax.ShapeDtypeStruct((rows, w), jnp.bfloat16) for _, w in ranges],
        compiler_params=pltpu.CompilerParams(vmem_limit_bytes=LIMIT),
    )(mask[None, :], weights[None, :], cot)


def select_kernel(base, rows, plan_ref, masks_ref, *refs):
    parts, (out_ref, most_ref) = refs[:-2], refs[-2:]
    kept = jnp.sum(masks_ref[...].astype(jnp.float32), axis=1, keepdims=True)
    most_ref[...] = jnp.broadcast_to(jnp.max(kept, axis=0, keepdims=True), most_ref.shape)
    per = masks_ref.shape[1]
    got, at = [], 0
    for part in parts:
        for b in range(part.shape[0] // per):
            pick = picker(masks_ref[pl.ds(plan_ref[2 * plan_ref.shape[0] // 3 + at], 1), :], base, rows)
            block = part[b * per : (b + 1) * per, :]
            got.append(jnp.dot(pick, block, preferred_element_type=jnp.float32))
            at += 1
    out_ref[...] = jnp.concatenate(got, axis=0).T.astype(jnp.bfloat16)


def select(parts, masks, plan, base, rows):
    features = parts[0].shape[1]
    tile = tile_of(0, features, 384)
    if features % tile:
        tile = features
    owners = masks.shape[0]
    return pl.pallas_call(
        functools.partial(select_kernel, base, rows),
        grid_spec=pltpu.PrefetchScalarGridSpec(
            num_scalar_prefetch=1,
            grid=(features // tile,),
            in_specs=[pl.BlockSpec(masks.shape, lambda i, plan: (0, 0))]
            + [pl.BlockSpec((p.shape[0], tile), lambda i, plan: (0, i)) for p in parts],
            out_specs=[
                pl.BlockSpec((tile, owners * rows), lambda i, plan: (i, 0)),
                pl.BlockSpec((8, LANES), lambda i, plan: (0, 0)),
            ],
        ),
        out_shape=[
            jax.ShapeDtypeStruct((features, owners * rows), jnp.bfloat16),
            jax.ShapeDtypeStruct((8, LANES), jnp.float32),
        ],
        compiler_params=pltpu.CompilerParams(vmem_limit_bytes=LIMIT),
    )(plan, masks, *parts)


def join_kernel(one_ref, two_ref, out_ref):
    out_ref[...] = jnp.concatenate([one_ref[...], two_ref[...]], axis=0)


def join(one, two):
    return pl.pallas_call(
        join_kernel,
        out_shape=jax.ShapeDtypeStruct((2 * one.shape[0], one.shape[1]), one.dtype),
        compiler_params=pltpu.CompilerParams(vmem_limit_bytes=2**20),
    )(one, two)


def product_kernel(n, cap, rows, adds, line, plan_ref, most_ref, panel_ref, *refs):
    pieces, (out_ref, mark_ref, depth_ref) = refs[:n], refs[-3:]
    i = pl.program_id(1)
    mark_ref[...] = most_ref[...]

    @pl.when(i == 0)
    def _():
        for j in range(n):
            depth_ref[pl.ds(pl.multiple_of(plan_ref[line * n + j] * cap, 16), cap), :] = pieces[j][...]

    panel = panel_ref[pl.ds(pl.multiple_of(i * rows, 16), rows), :]
    result = jnp.dot(panel, depth_ref[...], preferred_element_type=jnp.float32)
    if adds:
        result = result + refs[n][...]
    out_ref[...] = result


def product(panel_t, most, pieces, plan, line, out, adds, first, shape):
    n, (cap, width) = len(pieces), pieces[0].shape
    features, depth = panel_t.shape
    blocks = 3 if features % (3 * 16) == 0 else 1
    rows = features // blocks
    tile = tile_of(first, width, 768 if adds else 1536)
    place = lambda j, i, plan: (i, first // tile + j)
    specs = [
        pl.BlockSpec((8, LANES), lambda j, i, plan: (0, 0)),
        pl.BlockSpec((features, depth), lambda j, i, plan: (0, 0)),
    ]
    specs += [pl.BlockSpec((cap, tile), lambda j, i, plan: (0, j)) for _ in pieces]
    args = [plan, most, panel_t, *pieces]
    aliases = {}
    if out is not None:
        specs.append(pl.BlockSpec((rows, tile), place) if adds else pl.BlockSpec(memory_space=pl.ANY))
        args.append(out)
        aliases = {len(args) - 1: 0}
    return pl.pallas_call(
        functools.partial(product_kernel, n, cap, rows, adds, line),
        grid_spec=pltpu.PrefetchScalarGridSpec(
            num_scalar_prefetch=1,
            grid=(width // tile, blocks),
            in_specs=specs,
            out_specs=[
                pl.BlockSpec((rows, tile), place),
                pl.BlockSpec((8, LANES), lambda j, i, plan: (0, 0)),
            ],
            scratch_shapes=[pltpu.VMEM((depth, tile), jnp.bfloat16)],
        ),
        out_shape=[
            jax.ShapeDtypeStruct(shape, jnp.float32),
            jax.ShapeDtypeStruct((8, LANES), jnp.float32),
        ],
        input_output_aliases=aliases,
        compiler_params=pltpu.CompilerParams(vmem_limit_bytes=LIMIT),
        cost_estimate=pl.CostEstimate(
            flops=2 * features * depth * width,
            bytes_accessed=features * (4 * width + 2 * depth) + 2 * depth * width,
            transcendentals=0,
        ),
    )(*args)


def after(value, *earlier):
    return lax.optimization_barrier((value, *earlier))[0]


def plans(n, cols, several):
    walk = cycle(n)
    table = np.zeros((n, cols, 3, n), np.int32)
    for me in range(n):
        for col in range(cols):
            turn = col if cols == 4 else 0
            place = walk.index(me)
            for s in range(n):
                for line, owner in enumerate((walk[(place - s) % n], walk[(place + s) % n])):
                    table[me, col, line, s] = ((owner // several) ^ turn) * several + owner % several
                table[me, col, 2, s] = (((s // several) ^ turn) * several + s % several) ^ me
    return jnp.asarray(table.reshape(n * cols, 3 * n))


def body(panel, mask, timesteps, cot_gate):
    n, cols = lax.axis_size("row"), lax.axis_size("col")
    me, col = lax.axis_index("row"), lax.axis_index("col")
    per, width = cot_gate.shape
    shape = (panel.shape[1], width)
    total = per * n
    weights = token_weights(mask, timesteps, me * per, total // timesteps.shape[0], total)
    walk = cycle(n)
    fore = [(walk[i], walk[(i + 1) % n]) for i in range(n)]
    back = [(b, a) for a, b in fore]

    several = panel.shape[0] // per
    plan = lax.dynamic_slice(plans(n, cols, several), (me * cols + col, 0), (1, 3 * n))[0]
    cot_gate = after(cot_gate, plan)

    def swap(value, axis, size, bit):
        return lax.ppermute(value, axis, [(i, i ^ bit) for i in range(size)])

    cap = min(ROWS, per)
    spans = chunks_of(width, SPLIT)
    chunks = len(spans[0])
    packed = [pack(cot_gate, mask, weights, 0, cap, (spans[0][k], spans[1][k])) for k in range(chunks)]
    rings = [[[fore_piece], [back_piece]] for fore_piece, back_piece in packed]
    out, masks, panel_t = None, mask[None, :], None
    parts = [panel]
    bit, before, marks = 1, [packed[0][0]], []
    last = (chunks - 1) * STAGGER + n + 1
    for r in range(1, last + 1):
        fresh = []
        for k in range(chunks):
            step = r - STAGGER * k
            if 1 <= step < n:
                for ring, perm in zip(rings[k], (fore, back)):
                    tied = marks + (before if TIGHT or step == 1 else [])
                    ring.append(lax.ppermute(after(ring[-1], *tied), "row", perm))
                    fresh.append(ring[-1])
        if bit < n:
            masks = join(masks, swap(after(masks, *before), "row", n, bit))
            fresh.append(masks)
            bit *= 2
        if r == 1 and cols == 4:
            parts.append(swap(after(panel, *before), "col", cols, 1))
            parts.append(swap(after(panel, *before), "col", cols, 2))
        elif r == 1:
            parts = [lax.all_gather(panel, "col", axis=0, tiled=True)]
        if r == max(n - 4, 2) and cols == 4:
            parts.append(swap(after(parts[2], *before), "col", cols, 1))
        marks = []
        if r == n - 2:
            panel_t, most = select(parts, after(masks, *before), plan, 0, cap)
            marks = [most]
        for k in range(chunks):
            side = r - STAGGER * k - n
            if 0 <= side < 2:
                pieces = rings[k][side]
                pieces = [after(pieces[0], *before), *pieces[1:]]
                out, most = product(panel_t, most, pieces, plan, side, out, False, spans[side][k][0], shape)
                marks.append(most)
        before = fresh or before
    if cap == per:
        return out

    def rest(i, out):
        cot, near, weight, *panels = lax.optimization_barrier((cot_gate, mask, weights, *parts, masks, i))[:-1]
        spans = chunks_of(width, (1,))
        left = pack(cot, near, weight, cap, per - cap, (spans[0][0], spans[1][0]))
        panel_t, mark = select(panels[:-1], panels[-1], plan, cap, per - cap)
        for piece, perm, line, span in zip(left, (fore, back), (0, 1), spans):
            pieces = [piece]
            for _ in range(n - 1):
                pieces.append(lax.ppermute(pieces[-1], "row", perm))
            out, mark = product(panel_t, mark, pieces, plan, line, out, True, span[0][0], shape)
        return out

    return lax.fori_loop(0, (most[0, 0] > cap).astype(jnp.int32), rest, out)


def solution(mesh):
    placed = (P("col", "row"), P("row"), P(), P("row", "col"))
    return jax.shard_map(
        body, mesh=mesh, in_specs=placed, out_specs=P("row", "col"), check_vma=False
    )
```

```python
import functools
import math

import jax
import jax.numpy as jnp
import numpy as np
from jax import lax
from jax.experimental import pallas as pl
from jax.experimental.pallas import tpu as pltpu
from jax.sharding import PartitionSpec as P

STEPS = 32
LANES = 128
ROWS = 80
SPLIT = (2, 4)
MASK_ROUND = 1
PANEL_ROUND = 2
STAGGER = 3
LIMIT = 28 * 2**20
WIDE_LIMIT = 40 * 2**20


def token_weights(mask, timesteps, first, seq_len, total):
    count = mask.shape[0]
    position = first + jnp.arange(count, dtype=jnp.int32)
    which = position // seq_len
    onehot = which[:, None] == jnp.arange(timesteps.shape[0], dtype=jnp.int32)[None, :]
    level = jnp.sum(jnp.where(onehot, timesteps[None, :], 0), axis=1)
    scale = 1.0 / math.sqrt(total)
    return mask.astype(jnp.float32) * (STEPS / (level + 1).astype(jnp.float32)) * scale


def cycle(n):
    fast = 1
    while fast * fast * 4 <= n:
        fast *= 2
    slow = n // fast
    walk = [z * fast for z in range(slow)]
    for i, z in enumerate(reversed(range(slow))):
        xs = range(1, fast) if i % 2 == 0 else reversed(range(1, fast))
        walk += [z * fast + x for x in xs]
    return walk


def chunks_of(width, split):
    tiles = width // LANES
    fore = (tiles + 1) // 2
    out = []
    for first, count in ((0, fore), (fore, tiles - fore)):
        if tiles % 2 or count % sum(split):
            split = (1,)
        ranges, at = [], first
        for part in split:
            size = part * (count // sum(split))
            ranges.append((at * LANES, size * LANES))
            at += size
        out.append(ranges)
    return out


def tile_of(first, width, most):
    best = LANES
    for size in range(LANES, most + 1, LANES):
        if first % size == 0 and width % size == 0:
            best = size
    return best


def picker(mask_row, base, rows):
    count = mask_row.shape[1]
    kept = jnp.broadcast_to(mask_row, (8, count)).astype(jnp.float32)
    before = lax.broadcasted_iota(jnp.int32, (count, count), 0)
    after = lax.broadcasted_iota(jnp.int32, (count, count), 1)
    upper = jnp.where(before <= after, 1.0, 0.0)
    rank = jnp.dot(kept.astype(jnp.bfloat16), upper.astype(jnp.bfloat16), preferred_element_type=jnp.float32)
    rank = jnp.where(kept > 0, rank, 0.0)[0:1]
    place = lax.broadcasted_iota(jnp.int32, (rows, count), 0) + (base + 1)
    return jnp.where(place.astype(jnp.float32) == rank, 1.0, 0.0).astype(jnp.bfloat16)


def pack_kernel(base, rows, unit, ranges, mask_ref, weight_ref, cot_ref, *outs):
    count = cot_ref.shape[0]
    pick = picker(mask_ref[...], base, rows)
    across = lax.broadcasted_iota(jnp.int32, (count, count), 0)
    along = lax.broadcasted_iota(jnp.int32, (count, count), 1)
    weight = jnp.sum(jnp.where(across == along, weight_ref[...], 0.0), axis=1, keepdims=True)
    weighted = (cot_ref[...].astype(jnp.float32) * weight).astype(jnp.bfloat16)
    packed = jnp.dot(pick, weighted, preferred_element_type=jnp.float32).astype(jnp.bfloat16)
    steps = [width // unit for _, width in ranges]
    for k, out in enumerate(outs):
        for u in range(steps[k]):

            @pl.when(pl.program_id(0) == sum(steps[:k]) + u)
            def _(out=out, u=u):
                out[:, u * unit : (u + 1) * unit] = packed


def pack(cot, mask, weights, base, rows, ranges):
    count = cot.shape[0]
    unit = functools.reduce(math.gcd, [v for r in ranges for v in r if v])
    (first, width), (second, other) = ranges
    steps = width // unit
    return pl.pallas_call(
        functools.partial(pack_kernel, base, rows, unit, ranges),
        grid=((width + other) // unit,),
        in_specs=[
            pl.BlockSpec((1, count), lambda i: (0, 0)),
            pl.BlockSpec((1, count), lambda i: (0, 0)),
            pl.BlockSpec(
                (count, unit),
                lambda i: (0, jnp.where(i < steps, first // unit + i, second // unit + i - steps)),
            ),
        ],
        out_specs=[pl.BlockSpec((rows, w), lambda i: (0, 0)) for _, w in ranges],
        out_shape=[jax.ShapeDtypeStruct((rows, w), jnp.bfloat16) for _, w in ranges],
        compiler_params=pltpu.CompilerParams(vmem_limit_bytes=LIMIT),
    )(mask[None, :], weights[None, :], cot)


def select_kernel(base, rows, plan_ref, masks_ref, *refs):
    parts, (out_ref, most_ref) = refs[:-2], refs[-2:]
    kept = jnp.sum(masks_ref[...].astype(jnp.float32), axis=1, keepdims=True)
    most_ref[...] = jnp.broadcast_to(jnp.max(kept, axis=0, keepdims=True), most_ref.shape)
    per = masks_ref.shape[1]
    got, at = [], 0
    for part in parts:
        for b in range(part.shape[0] // per):
            pick = picker(masks_ref[pl.ds(plan_ref[2 * plan_ref.shape[0] // 3 + at], 1), :], base, rows)
            block = part[b * per : (b + 1) * per, :]
            got.append(jnp.dot(pick, block, preferred_element_type=jnp.float32))
            at += 1
    out_ref[...] = jnp.concatenate(got, axis=0).T.astype(jnp.bfloat16)


def select(parts, masks, plan, base, rows):
    features = parts[0].shape[1]
    tile = tile_of(0, features, 384)
    if features % tile:
        tile = features
    owners = masks.shape[0]
    return pl.pallas_call(
        functools.partial(select_kernel, base, rows),
        grid_spec=pltpu.PrefetchScalarGridSpec(
            num_scalar_prefetch=1,
            grid=(features // tile,),
            in_specs=[pl.BlockSpec(masks.shape, lambda i, plan: (0, 0))]
            + [pl.BlockSpec((p.shape[0], tile), lambda i, plan: (0, i)) for p in parts],
            out_specs=[
                pl.BlockSpec((tile, owners * rows), lambda i, plan: (i, 0)),
                pl.BlockSpec((8, LANES), lambda i, plan: (0, 0)),
            ],
        ),
        out_shape=[
            jax.ShapeDtypeStruct((features, owners * rows), jnp.bfloat16),
            jax.ShapeDtypeStruct((8, LANES), jnp.float32),
        ],
        compiler_params=pltpu.CompilerParams(vmem_limit_bytes=LIMIT),
    )(plan, masks, *parts)


def join_kernel(one_ref, two_ref, out_ref):
    out_ref[...] = jnp.concatenate([one_ref[...], two_ref[...]], axis=0)


def join(one, two):
    return pl.pallas_call(
        join_kernel,
        out_shape=jax.ShapeDtypeStruct((2 * one.shape[0], one.shape[1]), one.dtype),
        compiler_params=pltpu.CompilerParams(vmem_limit_bytes=2**20),
    )(one, two)


def product_kernel(n, cap, rows, adds, lines, tiles, plan_ref, most_ref, panel_ref, *refs):
    out_ref, mark_ref, depth_ref = refs[-3:]
    j, i = pl.program_id(0), pl.program_id(1)
    mark_ref[...] = most_ref[...]
    for k, line in enumerate(lines):

        @pl.when((i == 0) & (j >= k * tiles) & (j < (k + 1) * tiles))
        def _(pieces=refs[k * n : (k + 1) * n], line=line):
            for s in range(n):
                at = pl.multiple_of(plan_ref[line * n + s] * cap, 16)
                depth_ref[pl.ds(at, cap), :] = pieces[s][...]

    panel = panel_ref[pl.ds(pl.multiple_of(i * rows, 16), rows), :]
    result = jnp.dot(panel, depth_ref[...], preferred_element_type=jnp.float32)
    if adds:
        result = result + refs[len(lines) * n][...]
    out_ref[...] = result


def product(panel_t, most, sides, plan, out, adds, shape):
    pieces, lines, firsts = zip(*sides)
    n, (cap, width) = len(pieces[0]), pieces[0][0].shape
    features, depth = panel_t.shape
    blocks = 3 if features % (3 * 16) == 0 else 1
    rows = features // blocks
    tile = min(tile_of(first, width, 768 if adds else 1536) for first in firsts)
    tiles = width // tile
    bases = [first // tile for first in firsts]

    def place(j, i, plan):
        column = bases[0] + j
        for k in range(1, len(bases)):
            column = jnp.where(j >= k * tiles, bases[k] + j - k * tiles, column)
        return i, column

    specs = [
        pl.BlockSpec((8, LANES), lambda j, i, plan: (0, 0)),
        pl.BlockSpec((features, depth), lambda j, i, plan: (0, 0)),
    ]
    for k in range(len(sides)):
        turn = lambda j, i, plan, k=k: (0, jnp.clip(j - k * tiles, 0, tiles - 1))
        specs += [pl.BlockSpec((cap, tile), turn)] * n
    args = [plan, most, panel_t, *sum(pieces, [])]
    aliases = {}
    if out is not None:
        specs.append(pl.BlockSpec((rows, tile), place) if adds else pl.BlockSpec(memory_space=pl.ANY))
        args.append(out)
        aliases = {len(args) - 1: 0}
    return pl.pallas_call(
        functools.partial(product_kernel, n, cap, rows, adds, lines, tiles),
        grid_spec=pltpu.PrefetchScalarGridSpec(
            num_scalar_prefetch=1,
            grid=(len(sides) * tiles, blocks),
            in_specs=specs,
            out_specs=[
                pl.BlockSpec((rows, tile), place),
                pl.BlockSpec((8, LANES), lambda j, i, plan: (0, 0)),
            ],
            scratch_shapes=[pltpu.VMEM((depth, tile), jnp.bfloat16)],
        ),
        out_shape=[
            jax.ShapeDtypeStruct(shape, jnp.float32),
            jax.ShapeDtypeStruct((8, LANES), jnp.float32),
        ],
        input_output_aliases=aliases,
        compiler_params=pltpu.CompilerParams(vmem_limit_bytes=LIMIT if len(sides) == 1 else WIDE_LIMIT),
        cost_estimate=pl.CostEstimate(
            flops=2 * features * depth * width * len(sides),
            bytes_accessed=(features * 4 + 2 * depth) * width * len(sides) + 2 * features * depth,
            transcendentals=0,
        ),
    )(*args)


def after(value, *earlier):
    return lax.optimization_barrier((value, *earlier))[0]


def plans(n, cols, several):
    walk = cycle(n)
    table = np.zeros((n, cols, 3, n), np.int32)
    for me in range(n):
        for col in range(cols):
            turn = col if cols == 4 else 0
            place = walk.index(me)
            for s in range(n):
                for line, owner in enumerate((walk[(place - s) % n], walk[(place + s) % n])):
                    table[me, col, line, s] = ((owner // several) ^ turn) * several + owner % several
                table[me, col, 2, s] = (((s // several) ^ turn) * several + s % several) ^ me
    return jnp.asarray(table.reshape(n * cols, 3 * n))


def body(panel, mask, timesteps, cot_gate):
    n, cols = lax.axis_size("row"), lax.axis_size("col")
    me, col = lax.axis_index("row"), lax.axis_index("col")
    per, width = cot_gate.shape
    shape = (panel.shape[1], width)
    total = per * n
    weights = token_weights(mask, timesteps, me * per, total // timesteps.shape[0], total)
    walk = cycle(n)
    fore = [(walk[i], walk[(i + 1) % n]) for i in range(n)]
    back = [(b, a) for a, b in fore]

    several = panel.shape[0] // per
    plan = lax.dynamic_slice(plans(n, cols, several), (me * cols + col, 0), (1, 3 * n))[0]
    cot_gate = after(cot_gate, plan)

    def swap(value, axis, size, bit):
        return lax.ppermute(value, axis, [(i, i ^ bit) for i in range(size)])

    cap = min(ROWS, per)
    spans = chunks_of(width, SPLIT)
    chunks = len(spans[0])
    packed = [pack(cot_gate, mask, weights, 0, cap, (spans[0][k], spans[1][k])) for k in range(chunks)]
    rings = [[[fore_piece], [back_piece]] for fore_piece, back_piece in packed]
    out, masks, panel_t = None, mask[None, :], None
    parts = [panel]
    bit, before, marks = 1, [packed[0][0]], []
    last = (chunks - 1) * STAGGER + n + 1
    for r in range(1, last + 1):
        fresh = []
        for k in range(chunks):
            step = r - STAGGER * k
            if 1 <= step < n:
                for ring, perm in zip(rings[k], (fore, back)):
                    tied = marks + before
                    ring.append(lax.ppermute(after(ring[-1], *tied), "row", perm))
                    fresh.append(ring[-1])
        if bit < n and r >= MASK_ROUND:
            masks = join(masks, swap(after(masks, *before), "row", n, bit))
            fresh.append(masks)
            bit *= 2
        if r == PANEL_ROUND and cols == 4:
            parts.append(swap(after(panel, *before), "col", cols, 1))
            parts.append(swap(after(panel, *before), "col", cols, 2))
        elif r == PANEL_ROUND:
            parts = [lax.all_gather(panel, "col", axis=0, tiled=True)]
        if r == max(n - 3, 2) and cols == 4:
            parts.append(swap(after(parts[2], *before), "col", cols, 1))
        marks = []
        if r == n - 1:
            panel_t, most = select(parts, after(masks, *before), plan, 0, cap)
            marks = [most]
        for k in range(chunks):
            due = r - STAGGER * k - n
            sides = [(rings[k][side], side, spans[side][k][0]) for side in range(2)]
            if k < chunks - 1 or spans[0][k][1] != spans[1][k][1]:
                sides = sides[due : due + 1]
            if sides and 0 <= due < 3 - len(sides):
                pieces = sides[0][0]
                sides[0] = ([after(pieces[0], *before), *pieces[1:]], *sides[0][1:])
                out, most = product(panel_t, most, sides, plan, out, False, shape)
                marks.append(most)
        before = fresh or before
    if cap == per:
        return out

    def rest(i, out):
        cot, near, weight, *panels = lax.optimization_barrier((cot_gate, mask, weights, *parts, masks, i))[:-1]
        spans = chunks_of(width, (1,))
        left = pack(cot, near, weight, cap, per - cap, (spans[0][0], spans[1][0]))
        panel_t, mark = select(panels[:-1], panels[-1], plan, cap, per - cap)
        for piece, perm, line, span in zip(left, (fore, back), (0, 1), spans):
            pieces = [piece]
            for _ in range(n - 1):
                pieces.append(lax.ppermute(pieces[-1], "row", perm))
            out, mark = product(panel_t, mark, [(pieces, line, span[0][0])], plan, out, True, shape)
        return out

    return lax.fori_loop(0, (most[0, 0] > cap).astype(jnp.int32), rest, out)


def solution(mesh):
    placed = (P("col", "row"), P("row"), P(), P("row", "col"))
    return jax.shard_map(
        body, mesh=mesh, in_specs=placed, out_specs=P("row", "col"), check_vma=False
    )
```
